256 devices in a mesh: row: 8 (over z_lo, core), col: 32 (over y, z_hi, x).
Axes of the slice: x: 4, y: 4, z: 8 (z_hi: 2, z_lo: 4; z = z_hi * 4 + z_lo), core: 2. Of those that a mesh axis runs over, the one named last changes fastest.
Arguments:
- activations: bfloat16 [1024, 8192], P(('row', 'col')), may hold values from -6 to 6
- cotangent: bfloat16 [1024, 8192], P(('row', 'col')), may hold values from -1.5 to 1.5
- up_panels: bfloat16 [16, 128, 128, 128], P('row', 'col'), may hold values from -0.125 to 0.125
- down_panels: bfloat16 [16, 128, 128, 128], P('row', 'col'), may hold values from -0.09375 to 0.09375
- block_index: int32 [128, 16], P('col'), may hold values from 0 to 63, as said below
- block_count: int32 [128], P('col'), may hold values from 5 to 16, as said below
Outputs:
- outputs: bfloat16 [1024, 8192], P(('row', 'col'))
- grad_inputs: bfloat16 [1024, 8192], P(('row', 'col'))
- grad_up: bfloat16 [16, 128, 128, 128], P('row', 'col')
- grad_down: bfloat16 [16, 128, 128, 128], P('row', 'col')
The draws below stay inside these ranges and needn't reach their ends.
Inputs may be any that keep to these rules, and one draw needn't show every extreme that they name: `block_index`: the 16 block numbers of one panel are distinct. `block_count`: some panel has all 16 slots live.
All inputs are finite; a program needn't handle non-finite values.
Results may differ from the reference program's by a relative error of at most 0.024.
Values may be sent and summed in bfloat16 or wider, within the bound.
No kernel may reach another device: no remote copies, remote signals or barrier semaphores. Data moves between devices by JAX's collectives and lax.ppermute only.
A program may use at most 128 MiB of HBM per device.

```python
import jax
import jax.numpy as jnp
from jax import lax

D = 8192
F = 16384
BLK = 128
KMAX = 16
TOK_ROW = 128
DB = 64
PANELS = 128
TOKENS = 1024
N_ROW = 8
N_COL = 32


def draw_block_index(key, part):
    key = jax.random.fold_in(key, 11)
    panel_keys = jax.random.split(key, PANELS)
    orders = jax.vmap(lambda one_key: jax.random.permutation(one_key, DB))(panel_keys)
    return orders[:, :KMAX].astype(jnp.int32)


def draw_block_count(key, part):
    key = jax.random.fold_in(key, 23)
    first_key, second_key = jax.random.split(key)
    counted = jax.random.randint(first_key, (PANELS,), KMAX // 3, KMAX + 1)
    fullest = jax.random.randint(second_key, (), 0, PANELS)
    positions = jnp.arange(PANELS, dtype=jnp.int32)
    return jnp.where(positions == fullest, KMAX, counted).astype(jnp.int32)


def block_scale(own_key, dims, shards, low, top_value):
    gain = 1.0
    for axis_at, parts in shards:
        heights = jax.random.uniform(jax.random.fold_in(jax.random.fold_in(own_key, 6), axis_at), (parts,), jnp.float32, low / len(shards), top_value / len(shards))
        gain = gain * jnp.repeat(jnp.exp(heights), dims[axis_at] // parts).reshape((-1,) + (1,) * (len(dims) - 1 - axis_at))
    return gain


def scatter_about(own_key, dims, scale, bound, cuts=(), kind=jnp.bfloat16):
    drawn = scale * jax.random.normal(own_key, dims, jnp.float32)
    if cuts:
        drawn = drawn * block_scale(own_key, dims, cuts, -0.22, 0.18)
    return jnp.clip(drawn, -bound, bound).astype(kind)


def setup_inputs(seed: int = 0) -> dict:
    keys = jax.random.split(jax.random.key(seed), 7)
    activations = scatter_about(keys[0], (TOKENS, D), 1.0, 6.0, ((0, 256),))
    cotangent = scatter_about(keys[1], (TOKENS, D), 0.25, 1.5, ((0, 256),))
    up_panels = scatter_about(keys[2], (KMAX, PANELS, BLK, BLK), (D // 4) ** -0.5, 0.125, ((0, 8), (1, 32)))
    down_panels = scatter_about(keys[3], (KMAX, PANELS, BLK, BLK), (F // 4) ** -0.5, 0.09375, ((0, 8), (1, 32)))
    block_index = draw_block_index(jax.random.fold_in(keys[6], 71), 0)
    block_count = draw_block_count(jax.random.fold_in(keys[6], 71), 0)
    return {"activations": activations, "cotangent": cotangent, "up_panels": up_panels, "down_panels": down_panels, "block_index": block_index, "block_count": block_count}


def select_blocks(matrix, indices, panels, slot_count):
    row_count = matrix.shape[0]
    blocked = matrix.reshape(row_count, matrix.shape[1] // BLK, BLK)
    return jnp.take(blocked, indices, axis=1).reshape(row_count, panels, slot_count, BLK)


def round_trip(partial_sum):
    rounded = lax.optimization_barrier(partial_sum.astype(jnp.bfloat16))
    return rounded.astype(jnp.float32)


def reference(activations, cotangent, up_panels, down_panels, block_index, block_count):
    highest = lax.Precision.HIGHEST
    active = jnp.arange(KMAX, dtype=jnp.int32)[:, None] < block_count[None, :]
    nothing = jnp.zeros((), jnp.bfloat16)
    up_blocks = jnp.where(active[:, :, None, None], up_panels, nothing)
    down_blocks = jnp.where(active[:, :, None, None], down_panels, nothing)
    per_group = PANELS // N_COL
    up_groups = up_blocks.reshape(KMAX, N_COL, per_group, BLK, BLK).transpose(1, 0, 2, 3, 4)
    down_groups = down_blocks.reshape(KMAX, N_COL, per_group, BLK, BLK).transpose(1, 0, 2, 3, 4)
    index_groups = block_index.reshape(N_COL, per_group, KMAX)
    active_groups = active.reshape(KMAX, N_COL, per_group).transpose(1, 0, 2)

    def one_group(running, group_items):
        out_sum, in_sum = running
        up_here, down_here, index_here, active_here = group_items
        indices = index_here.reshape(-1).astype(jnp.int32)
        selector = (indices[:, None] == jnp.arange(DB, dtype=jnp.int32)[None, :]).astype(jnp.float32)
        selector = selector.reshape(per_group, KMAX, DB)
        act_blocks = select_blocks(activations, indices, per_group, KMAX).astype(jnp.float32)
        cot_blocks = select_blocks(cotangent, indices, per_group, KMAX).astype(jnp.float32)
        up_float = up_here.astype(jnp.float32)
        down_float = down_here.astype(jnp.float32)
        preact = jnp.einsum("tpkd,kpdc->tpc", act_blocks, up_float, precision=highest)
        gate_value = jax.nn.sigmoid(preact)
        hidden = (preact * gate_value).astype(jnp.bfloat16)
        derivative = gate_value * (1.0 + preact * (1.0 - gate_value))
        grad_hidden = jnp.einsum("tpku,kpcu->tpc", cot_blocks, down_float, precision=highest)
        grad_pre = (grad_hidden * derivative).astype(jnp.bfloat16)
        hidden_float = hidden.astype(jnp.float32)
        grad_float = grad_pre.astype(jnp.float32)
        spread = jnp.einsum("tpc,kpcu->tpku", hidden_float, down_float, precision=highest)
        out_part = jnp.einsum("tpku,pkb->tbu", spread, selector, precision=highest).reshape(TOKENS, D)
        spread_in = jnp.einsum("tpc,kpdc->tpkd", grad_float, up_float, precision=highest)
        in_part = jnp.einsum("tpkd,pkb->tbd", spread_in, selector, precision=highest).reshape(TOKENS, D)
        act_rows = act_blocks.reshape(N_ROW, TOK_ROW, per_group, KMAX, BLK)
        cot_rows = cot_blocks.reshape(N_ROW, TOK_ROW, per_group, KMAX, BLK)
        grad_rows = grad_float.reshape(N_ROW, TOK_ROW, per_group, BLK)
        hidden_rows = hidden_float.reshape(N_ROW, TOK_ROW, per_group, BLK)
        mask = active_here[None, :, :, None, None]
        up_part = jnp.einsum("rtpkd,rtpc->rkpdc", act_rows, grad_rows, precision=highest)
        down_part = jnp.einsum("rtpc,rtpku->rkpcu", hidden_rows, cot_rows, precision=highest)
        up_part = jnp.where(mask, up_part, jnp.zeros((), jnp.float32))
        down_part = jnp.where(mask, down_part, jnp.zeros((), jnp.float32))
        up_grad = jnp.sum(round_trip(up_part), axis=0).astype(jnp.bfloat16)
        down_grad = jnp.sum(round_trip(down_part), axis=0).astype(jnp.bfloat16)
        return (out_sum + round_trip(out_part), in_sum + round_trip(in_part)), (up_grad, down_grad)

    start_sums = (jnp.zeros((TOKENS, D), jnp.float32), jnp.zeros((TOKENS, D), jnp.float32))
    sums, grads = lax.scan(one_group, start_sums, (up_groups, down_groups, index_groups, active_groups))
    grad_up = grads[0].transpose(1, 0, 2, 3, 4).reshape(KMAX, PANELS, BLK, BLK)
    grad_down = grads[1].transpose(1, 0, 2, 3, 4).reshape(KMAX, PANELS, BLK, BLK)
    return (sums[0].astype(jnp.bfloat16), sums[1].astype(jnp.bfloat16), grad_up, grad_down)
```

```python
import functools

import jax
import jax.numpy as jnp
from jax import lax
from jax.experimental import pallas as pl
from jax.experimental.pallas import tpu as pltpu
from jax.sharding import PartitionSpec as P

BLK = 128
NX, NY, NZ = 4, 4, 2
BF = jnp.bfloat16
F32 = jnp.float32
NT = (((1,), (1,)), ((), ()))
TN = (((0,), (0,)), ((), ()))


def col_index(y, z, x):
    return ((y % NY) * NZ + z % NZ) * NX + x % NX


def send(value, dy, dz, dx):
    pairs = [
        (col_index(y, z, x), col_index(y + dy, z + dz, x + dx))
        for y in range(NY)
        for z in range(NZ)
        for x in range(NX)
    ]
    return lax.ppermute(value, "col", pairs)


def fetch(value, dy, dz, dx):
    return send(value, -dy, -dz, -dx)


def block_kernel(slots, panels, *refs):
    index, count = refs[:2]
    act_in, cot_in, weights_in = refs[2:6], refs[6:10], refs[10]
    out_refs, gin_refs, grads = refs[11:15], refs[15:19], refs[19]
    act, cot, weights, out_sum, in_sum, a_cat, c_cat, up_cat, down_cat, sems = refs[20:]
    copies = []
    for d in range(4):
        copies.append(pltpu.make_async_copy(act_in[d], act.at[d], sems.at[d]))
        copies.append(pltpu.make_async_copy(cot_in[d], cot.at[:, d], sems.at[4 + d]))
    copies.append(pltpu.make_async_copy(weights_in, weights, sems.at[8]))
    for copy in copies:
        copy.start()
    out_sum[...] = jnp.zeros_like(out_sum)
    in_sum[...] = jnp.zeros_like(in_sum)
    for copy in copies:
        copy.wait()
    rows = act.shape[0] * act.shape[1] * act.shape[2]

    def one_panel(p, carry):
        live = count[p]
        for k in range(slots):
            r, s = k // 2, k % 2
            lanes = pl.ds(pl.multiple_of(index[p, k] * BLK, BLK), BLK)
            here = slice(k * BLK, (k + 1) * BLK)
            a_cat[:, here] = act[:, :, :, lanes].reshape(rows, BLK)
            c_cat[:, here] = cot[:, :, :, lanes].reshape(rows, BLK)
            up = weights[r, 0, s, p]
            down = weights[r, 1, s, p]
            up_cat[here, :] = jnp.where(k < live, up, jnp.zeros_like(up))
            down_cat[:, here] = jnp.where(k < live, down, jnp.zeros_like(down))
        preact = jnp.dot(a_cat[...], up_cat[...], preferred_element_type=F32)
        gate = jax.nn.sigmoid(preact)
        hidden = (preact * gate).astype(BF)
        derivative = gate * (1.0 + preact * (1.0 - gate))
        grad_hidden = lax.dot_general(c_cat[...], down_cat[...], NT, preferred_element_type=F32)
        grad_pre = (grad_hidden * derivative).astype(BF)
        spread = jnp.dot(hidden, down_cat[...], preferred_element_type=F32)
        spread_in = lax.dot_general(grad_pre, up_cat[...], NT, preferred_element_type=F32)
        up_grad = lax.dot_general(a_cat[...], grad_pre, TN, preferred_element_type=F32)
        down_grad = lax.dot_general(hidden, c_cat[...], TN, preferred_element_type=F32)
        for k in range(slots):
            r, s = k // 2, k % 2
            lanes = pl.ds(pl.multiple_of(index[p, k] * BLK, BLK), BLK)
            here = slice(k * BLK, (k + 1) * BLK)
            out_sum[:, lanes] += spread[:, here]
            in_sum[:, lanes] += spread_in[:, here]
            up_here, down_here = up_grad[here, :], down_grad[:, here]
            grads[r, 0, s, p] = jnp.where(k < live, up_here, 0.0).astype(BF)
            grads[r, 1, s, p] = jnp.where(k < live, down_here, 0.0).astype(BF)
        return carry

    lax.fori_loop(0, panels, one_panel, 0)
    for d in range(4):
        for e in range(4):
            place = pl.ds((d * 4 + e) * 8, 8)
            out_refs[d][e] = out_sum[place, :].astype(BF)
            gin_refs[e][d] = in_sum[place, :].astype(BF)


def block_products(index, count, act_parts, cot_parts, weights):
    panels, slots = index.shape
    part = act_parts[0].shape
    features = part[-1]
    rows = 4 * part[0] * part[1]
    any_space = pl.BlockSpec(memory_space=pl.ANY)
    smem = pl.BlockSpec(memory_space=pltpu.SMEM)
    vmem = pl.BlockSpec(memory_space=pltpu.VMEM)
    return pl.pallas_call(
        functools.partial(block_kernel, slots, panels),
        out_shape=[jax.ShapeDtypeStruct(part, BF)] * 8 + [jax.ShapeDtypeStruct(weights.shape, BF)],
        in_specs=[smem, smem] + [any_space] * 9,
        out_specs=[vmem] * 9,
        scratch_shapes=[
            pltpu.VMEM((4,) + part, BF),
            pltpu.VMEM((4,) + part, BF),
            pltpu.VMEM(weights.shape, BF),
            pltpu.VMEM((rows, features), F32),
            pltpu.VMEM((rows, features), F32),
            pltpu.VMEM((rows, slots * BLK), BF),
            pltpu.VMEM((rows, slots * BLK), BF),
            pltpu.VMEM((slots * BLK, BLK), BF),
            pltpu.VMEM((BLK, slots * BLK), BF),
            pltpu.SemaphoreType.DMA((9,)),
        ],
        compiler_params=pltpu.CompilerParams(vmem_limit_bytes=52 * 2**20),
        cost_estimate=pl.CostEstimate(flops=1_700_000_000, bytes_accessed=17_000_000, transcendentals=65536),
    )(index, count, *act_parts, *cot_parts, weights)


def total(terms):
    result = terms[0].astype(F32)
    for term in terms[1:]:
        result = result + term.astype(F32)
    return result


def shards(activations, cotangent, up_panels, down_panels, block_index, block_count):
    own_slots, panels = up_panels.shape[:2]
    own_weights = jnp.concatenate([up_panels.reshape(-1, BLK), down_panels.reshape(-1, BLK)])
    weights = lax.all_gather(own_weights, "row", axis=0, tiled=True)
    weights = weights.reshape(-1, 2, own_slots, panels, BLK, BLK)

    far = fetch(jnp.stack([activations, cotangent]), 0, 1, 0)
    act = jnp.concatenate([activations, far[0]])
    cot = jnp.concatenate([cotangent, far[1]])
    act = jnp.stack([act] + [fetch(act, 0, 0, d) for d in (1, 2, 3)])
    cot = jnp.stack([cot] + [fetch(cot, d, 0, 0) for d in (1, 2, 3)])
    act_parts = [act] + [fetch(act, d, 0, 0) for d in (1, 2, 3)]
    cot_parts = [cot] + [fetch(cot, 0, 0, d) for d in (1, 2, 3)]

    results = block_products(block_index, block_count, act_parts, cot_parts, weights)
    out_parts, in_parts, grads = results[:4], results[4:8], results[8]

    shares = lax.psum_scatter(grads.reshape(-1, BLK), "row", scatter_dimension=0, tiled=True)
    shares = shares.reshape(2, own_slots, panels, BLK, BLK)

    out = total([out_parts[0]] + [send(out_parts[d], d, 0, 0) for d in (1, 2, 3)]).astype(BF)
    gin = total([in_parts[0]] + [send(in_parts[d], 0, 0, d) for d in (1, 2, 3)]).astype(BF)
    out = total([out[0]] + [send(out[d], 0, 0, d) for d in (1, 2, 3)]).astype(BF)
    gin = total([gin[0]] + [send(gin[d], d, 0, 0) for d in (1, 2, 3)]).astype(BF)
    far = send(jnp.stack([out[4:], gin[4:]]), 0, 1, 0)
    outputs = total([out[:4], far[0]]).astype(BF)
    grad_inputs = total([gin[:4], far[1]]).astype(BF)
    return outputs, grad_inputs, shares[0], shares[1]


def solution(mesh):
    tokens = P(("row", "col"), None)
    blocks = P("row", "col", None, None)
    in_specs = (tokens, tokens, blocks, blocks, P("col", None), P("col"))
    out_specs = (tokens, tokens, blocks, blocks)
    return jax.shard_map(shards, mesh=mesh, in_specs=in_specs, out_specs=out_specs, check_vma=False)
```

```python
import functools

import jax
import jax.numpy as jnp
from jax import lax
from jax.experimental import pallas as pl
from jax.experimental.pallas import tpu as pltpu
from jax.sharding import PartitionSpec as P

BLK = 128
NX, NY, NH, NL, NC = 4, 4, 2, 4, 2
NZ = NH * NL
BF = jnp.bfloat16
F32 = jnp.float32
NT = (((1,), (1,)), ((), ()))
TN = (((0,), (0,)), ((), ()))
HOPS = (0, 1, 2, 3, -1, -2, -3, 4)


def device(z, core, y, x):
    z = z % NZ
    row = (z % NL) * NC + core % NC
    col = ((y % NY) * NH + z // NL) * NX + x % NX
    return row * NY * NH * NX + col


def send(value, dz=0, dc=0, dy=0, dx=0):
    pairs = [
        (device(z, c, y, x), device(z + dz, c + dc, y + dy, x + dx))
        for z in range(NZ)
        for c in range(NC)
        for y in range(NY)
        for x in range(NX)
    ]
    return lax.ppermute(value, ("row", "col"), pairs)


def swap_cores(value):
    return send(value, dc=1)


def total(terms):
    result = terms[0].astype(F32)
    for term in terms[1:]:
        result = result + term.astype(F32)
    return result


def row_swap(rows):
    i = lax.broadcasted_iota(jnp.int32, (rows, rows), 0)
    j = lax.broadcasted_iota(jnp.int32, (rows, rows), 1)
    other = (i // 64) * 64 + ((i // 4) % 4) * 16 + ((i // 16) % 4) * 4 + i % 4
    return other == j


def grads_kernel(slots, *refs):
    place, index, count = refs[:3]
    act_in, cot_in = refs[3:5], refs[5:7]
    weights_in = refs[7:16]
    grad_refs = refs[16:24]
    hidden_out, grad_out, up_out, down_out = refs[24:28]
    act, cot, weights, grads, a_cat, c_cat, sems = refs[28:]
    half = act.shape[0] // 2
    z = place[0]
    copies = []
    for o in range(2):
        span = pl.ds(o * half, half)
        copies.append(pltpu.make_async_copy(act_in[o], act.at[span], sems.at[o]))
        copies.append(pltpu.make_async_copy(cot_in[o], cot.at[span], sems.at[2 + o]))
    for n, hop in enumerate(HOPS[:7]):
        copies.append(pltpu.make_async_copy(weights_in[n], weights.at[(z + hop + NZ) % NZ], sems.at[4 + n]))
    for o in range(2):
        spot = weights.at[(z + 4) % NZ, pl.ds(4 * o, 4)]
        copies.append(pltpu.make_async_copy(weights_in[7 + o], spot, sems.at[11 + o]))
    for copy in copies:
        copy.start()
    swapped = row_swap(act.shape[0])
    swap_f, swap_b = swapped.astype(F32), swapped.astype(BF)
    for copy in copies:
        copy.wait()

    def one_panel(p, carry):
        live = count[p]
        for k in range(slots):
            lanes = pl.ds(pl.multiple_of(index[p, k] * BLK, BLK), BLK)
            here = slice(k * BLK, (k + 1) * BLK)
            a_cat[:, here] = act[:, lanes]
            c_cat[:, here] = cot[:, lanes]
            up = weights[p * NL + k // 4, k % 4 * 2]
            down = weights[p * NL + k // 4, k % 4 * 2 + 1]
            up_out[p, here, :] = jnp.where(k < live, up, jnp.zeros_like(up))
            down_out[p, :, here] = jnp.where(k < live, down, jnp.zeros_like(down))
        preact = jnp.dot(a_cat[...], up_out[p], preferred_element_type=F32)
        gate = jax.nn.sigmoid(preact)
        hidden = (preact * gate).astype(BF)
        derivative = gate * (1.0 + preact * (1.0 - gate))
        grad_hidden = lax.dot_general(c_cat[...], down_out[p], NT, preferred_element_type=F32)
        grad_hidden = jnp.dot(
            swap_f, grad_hidden, precision=lax.Precision.HIGHEST, preferred_element_type=F32
        )
        grad_pre = (grad_hidden * derivative).astype(BF)
        hidden_x = jnp.dot(swap_b, hidden, preferred_element_type=F32).astype(BF)
        grad_x = jnp.dot(swap_b, grad_pre, preferred_element_type=F32).astype(BF)
        hidden_out[p] = hidden
        grad_out[p] = grad_x
        up_grad = lax.dot_general(a_cat[...], grad_pre, TN, preferred_element_type=F32)
        down_grad = lax.dot_general(hidden_x, c_cat[...], TN, preferred_element_type=F32)
        for k in range(slots):
            here = slice(k * BLK, (k + 1) * BLK)
            grads[p * NL + k // 4, k % 4 * 2] = jnp.where(k < live, up_grad[here, :], 0.0).astype(BF)
            grads[p * NL + k // 4, k % 4 * 2 + 1] = jnp.where(k < live, down_grad[:, here], 0.0).astype(BF)
        return carry

    lax.fori_loop(0, NH, one_panel, 0)
    copies = [
        pltpu.make_async_copy(grads.at[(z + hop + NZ) % NZ], grad_refs[n], sems.at[n])
        for n, hop in enumerate(HOPS)
    ]
    for copy in copies:
        copy.start()
    for copy in copies:
        copy.wait()


def weight_grads(place, index, count, act_pair, cot_pair, weights):
    panels, slots = index.shape
    half, features = act_pair[0].shape
    shard = weights[0].shape
    any_space = pl.BlockSpec(memory_space=pl.ANY)
    smem = pl.BlockSpec(memory_space=pltpu.SMEM)
    vmem = pl.BlockSpec(memory_space=pltpu.VMEM)
    rows, wide = 2 * half, slots * BLK
    shapes = [shard] * NZ + [(panels, rows, BLK)] * 2 + [(panels, wide, BLK), (panels, BLK, wide)]
    results = pl.pallas_call(
        functools.partial(grads_kernel, slots),
        out_shape=[jax.ShapeDtypeStruct(shape, BF) for shape in shapes],
        in_specs=[smem] * 3 + [any_space] * 13,
        out_specs=[any_space] * NZ + [vmem] * 4,
        scratch_shapes=[
            pltpu.VMEM((rows, features), BF),
            pltpu.VMEM((rows, features), BF),
            pltpu.VMEM((NZ,) + shard, BF),
            pltpu.VMEM((NZ,) + shard, BF),
            pltpu.VMEM((rows, wide), BF),
            pltpu.VMEM((rows, wide), BF),
            pltpu.SemaphoreType.DMA((13,)),
        ],
        compiler_params=pltpu.CompilerParams(vmem_limit_bytes=32 * 2**20),
        cost_estimate=pl.CostEstimate(flops=600_000_000, bytes_accessed=12_000_000, transcendentals=32768),
    )(place, index, count, *act_pair, *cot_pair, *weights)
    return results[:NZ], results[NZ:]


def outputs_kernel(slots, index, *refs):
    sides, (out_own, out_far, in_own, in_far) = refs[:8], refs[8:12]
    out_sum, in_sum = refs[12:]
    out_sum[...] = jnp.zeros_like(out_sum)
    in_sum[...] = jnp.zeros_like(in_sum)
    for j in range(2):
        hidden, grad, ups, downs = sides[4 * j : 4 * j + 4]

        def one_panel(p, carry):
            spread = jnp.dot(hidden[p], downs[p], preferred_element_type=F32)
            spread_in = lax.dot_general(grad[p], ups[p], NT, preferred_element_type=F32)
            for k in range(slots):
                lanes = pl.ds(pl.multiple_of(index[2 * j + p, k] * BLK, BLK), BLK)
                here = slice(k * BLK, (k + 1) * BLK)
                out_sum[:, lanes] += spread[:, here]
                in_sum[:, lanes] += spread_in[:, here]
            return carry

        lax.fori_loop(0, NH, one_panel, 0)
    half = out_sum.shape[0] // 2
    out_own[...] = out_sum[:half, :].astype(BF)
    out_far[...] = out_sum[half:, :].astype(BF)
    in_own[...] = in_sum[:half, :].astype(BF)
    in_far[...] = in_sum[half:, :].astype(BF)


def output_sums(index, sides, half, features):
    slots = index.shape[1]
    smem = pl.BlockSpec(memory_space=pltpu.SMEM)
    vmem = pl.BlockSpec(memory_space=pltpu.VMEM)
    return pl.pallas_call(
        functools.partial(outputs_kernel, slots),
        out_shape=[jax.ShapeDtypeStruct((half, features), BF)] * 4,
        in_specs=[smem] + [vmem] * 8,
        out_specs=[vmem] * 4,
        scratch_shapes=[pltpu.VMEM((2 * half, features), F32)] * 2,
        compiler_params=pltpu.CompilerParams(vmem_limit_bytes=32 * 2**20),
        cost_estimate=pl.CostEstimate(flops=550_000_000, bytes_accessed=9_000_000, transcendentals=0),
    )(index, *sides)


def ring_gather(shard):
    up, down = [shard], [shard]
    for _ in range(3):
        up.append(send(up[-1], dz=-1))
        down.append(send(down[-1], dz=1))
    half = shard.shape[0] // 2
    across = [send(up[-1][:half], dz=-1), send(down[-1][half:], dz=1)]
    return [shard] + up[1:] + down[1:] + across


def ring_sum(parts):
    half = parts[7].shape[0] // 2
    first = total([parts[3][:half], send(parts[7][:half], dz=1)]).astype(BF)
    up = jnp.concatenate([first, parts[3][half:]])
    second = total([parts[6][half:], send(parts[7][half:], dz=-1)]).astype(BF)
    down = jnp.concatenate([parts[6][:half], second])
    for n in (2, 1):
        up = total([parts[n], send(up, dz=1)]).astype(BF)
        down = total([parts[3 + n], send(down, dz=-1)]).astype(BF)
    return total([parts[0], send(up, dz=1), send(down, dz=-1)]).astype(BF)


def gather_rows(value, **axis):
    ((name, _),) = axis.items()
    return jnp.concatenate([value] + [send(value, **{name: -d}) for d in (1, 2, 3)])


def sum_rows(own, far, first, second):
    far = swap_cores(far)
    rows = own.shape[0] // 4
    parts = [total([own[d * rows : (d + 1) * rows], far[d * rows : (d + 1) * rows]]) for d in range(4)]
    result = total(parts[:1] + [send(parts[d].astype(BF), **{first: d}) for d in (1, 2, 3)])
    rows = rows // 4
    parts = [result[d * rows : (d + 1) * rows] for d in range(4)]
    result = total(parts[:1] + [send(parts[d].astype(BF), **{second: d}) for d in (1, 2, 3)])
    return result.astype(BF)


def shards(activations, cotangent, up_panels, down_panels, block_index, block_count):
    row, col = lax.axis_index("row"), lax.axis_index("col")
    core, low, high = row % NC, row // NC, (col // NX) % NH
    own_first, low_half = core == 0, high == 0

    both = jnp.stack([up_panels, down_panels], axis=2)
    keep = lax.dynamic_slice_in_dim(both, 2 * core, 2, axis=1)
    got = swap_cores(lax.dynamic_slice_in_dim(both, 2 - 2 * core, 2, axis=1))
    slots_0, slots_1 = jnp.where(own_first, keep, got), jnp.where(own_first, got, keep)
    weights = []
    for j in range(2):
        shard = jnp.stack([slots_0[:, j], slots_1[:, j]]).reshape(-1, BLK, BLK)
        weights.append(ring_gather(shard))

    lists = jnp.concatenate([block_index, block_count[:, None]], axis=1)
    far_lists = send(lists, dz=4)
    lists = jnp.stack([jnp.where(low_half, lists, far_lists), jnp.where(low_half, far_lists, lists)], axis=1)
    lists = lax.dynamic_slice_in_dim(lists, 2 * core, 2, axis=0)
    index, count = lists[:, :, :-1], lists[:, :, -1]
    place = (high * NL + low).astype(jnp.int32).reshape(1)

    act = gather_rows(gather_rows(activations, dx=1), dy=1)
    cot = gather_rows(gather_rows(cotangent, dy=1), dx=1)
    act_pair, cot_pair = [act, swap_cores(act)], [cot, swap_cores(cot)]

    sides, sums = [], []
    for j in range(2):
        parts, side = weight_grads(place, index[j], count[j], act_pair, cot_pair, weights[j])
        sides.extend(side)
        sums.append(ring_sum(parts))
    out_own, out_far, in_own, in_far = output_sums(index.reshape(4, -1), sides, *act.shape)
    outputs = sum_rows(out_own, out_far, "dy", "dx")
    grad_inputs = sum_rows(in_own, in_far, "dx", "dy")

    mine, other = [], []
    for j in range(2):
        cores = sums[j].reshape(2, 2, 2, BLK, BLK)
        mine.append(lax.dynamic_index_in_dim(cores, core, 0, keepdims=False))
        other.append(swap_cores(lax.dynamic_index_in_dim(cores, 1 - core, 0, keepdims=False)))
    mine, other = jnp.stack(mine, axis=1), jnp.stack(other, axis=1)
    grads = jnp.where(
        own_first, jnp.concatenate([mine, other], axis=1), jnp.concatenate([other, mine], axis=1)
    )
    return outputs, grad_inputs, grads[:, :, 0], grads[:, :, 1]


def solution(mesh):
    tokens = P(("row", "col"), None)
    blocks = P("row", "col", None, None)
    in_specs = (tokens, tokens, blocks, blocks, P("col", None), P("col"))
    out_specs = (tokens, tokens, blocks, blocks)
    return jax.shard_map(shards, mesh=mesh, in_specs=in_specs, out_specs=out_specs, check_vma=False)
```

```python
import functools

import jax
import jax.numpy as jnp
from jax import lax
from jax.experimental import pallas as pl
from jax.experimental.pallas import tpu as pltpu
from jax.sharding import PartitionSpec as P

BLK = 128
NX, NY, NH, NL, NC = 4, 4, 2, 4, 2
NZ = NH * NL
BF = jnp.bfloat16
F32 = jnp.float32
NT = (((1,), (1,)), ((), ()))
TN = (((0,), (0,)), ((), ()))
HOPS = (0, 1, 2, 3, -1, -2, -3, 4)


def device(z, core, y, x):
    z = z % NZ
    row = (z % NL) * NC + core % NC
    col = ((y % NY) * NH + z // NL) * NX + x % NX
    return row * NY * NH * NX + col


def send(value, dz=0, dc=0, dy=0, dx=0):
    pairs = [
        (device(z, c, y, x), device(z + dz, c + dc, y + dy, x + dx))
        for z in range(NZ)
        for c in range(NC)
        for y in range(NY)
        for x in range(NX)
    ]
    return lax.ppermute(value, ("row", "col"), pairs)


def swap_cores(value):
    return send(value, dc=1)


def after(values, *others):
    return lax.optimization_barrier((values, others))[0]


def total(terms):
    result = terms[0].astype(F32)
    for term in terms[1:]:
        result = result + term.astype(F32)
    return result


def row_swap(rows):
    i = lax.broadcasted_iota(jnp.int32, (rows, rows), 0)
    j = lax.broadcasted_iota(jnp.int32, (rows, rows), 1)
    other = (i // 64) * 64 + ((i // 4) % 4) * 16 + ((i // 16) % 4) * 4 + i % 4
    return other == j


def products_kernel(slots, *refs):
    place, index, count = refs[:3]
    act_in, cot_in, weights_in = refs[3:5], refs[5:7], refs[7:16]
    grads_out, sums_out = refs[16:25], refs[25:29]
    act, cot, weights, grads, out_sum, in_sum, sums, a_cat, c_cat, up_cat, down_cat = refs[29:40]
    row_sems, weight_sems, grad_sems, sum_sems = refs[40:]
    rows = act.shape[0]
    half = rows // 2
    z = place[0]
    own = z // NL
    arrivals = []
    for o in range(2):
        span = pl.ds(o * half, half)
        arrivals.append(pltpu.make_async_copy(act_in[o], act.at[span], row_sems.at[o]))
        arrivals.append(pltpu.make_async_copy(cot_in[o], cot.at[span], row_sems.at[2 + o]))
    for n, hop in enumerate(HOPS[:7]):
        spot = weights.at[(z + hop + NZ) % NZ]
        arrivals.append(pltpu.make_async_copy(weights_in[n], spot, weight_sems.at[n]))
    for o in range(2):
        spot = weights.at[(z + 4) % NZ, pl.ds(8 * o, 8)]
        arrivals.append(pltpu.make_async_copy(weights_in[7 + o], spot, weight_sems.at[7 + o]))
    for copy in arrivals:
        copy.start()
    out_sum[...] = jnp.zeros_like(out_sum)
    in_sum[...] = jnp.zeros_like(in_sum)
    swapped = row_swap(rows)
    swap_f, swap_b = swapped.astype(F32), swapped.astype(BF)
    for copy in arrivals:
        copy.wait()

    def one_panel(n, carry):
        far, p = n // 2, n % 2
        base = jnp.where(far == 0, own, 1 - own) * NL
        live = count[n]
        for k in range(slots):
            lanes = pl.ds(pl.multiple_of(index[n, k] * BLK, BLK), BLK)
            here = slice(k * BLK, (k + 1) * BLK)
            a_cat[:, here] = act[:, lanes]
            c_cat[:, here] = cot[:, lanes]
            up = weights[base + k // 4, k % 4 * 4 + p * 2]
            down = weights[base + k // 4, k % 4 * 4 + p * 2 + 1]
            up_cat[here, :] = jnp.where(k < live, up, jnp.zeros_like(up))
            down_cat[:, here] = jnp.where(k < live, down, jnp.zeros_like(down))
        preact = jnp.dot(a_cat[...], up_cat[...], preferred_element_type=F32)
        gate = jax.nn.sigmoid(preact)
        hidden = (preact * gate).astype(BF)
        derivative = gate * (1.0 + preact * (1.0 - gate))
        grad_hidden = lax.dot_general(c_cat[...], down_cat[...], NT, preferred_element_type=F32)
        grad_hidden = jnp.dot(
            swap_f, grad_hidden, precision=lax.Precision.HIGHEST, preferred_element_type=F32
        )
        grad_pre = (grad_hidden * derivative).astype(BF)
        hidden_x = jnp.dot(swap_b, hidden, preferred_element_type=F32).astype(BF)
        grad_x = jnp.dot(swap_b, grad_pre, preferred_element_type=F32).astype(BF)
        up_grad = lax.dot_general(a_cat[...], grad_pre, TN, preferred_element_type=F32)
        down_grad = lax.dot_general(hidden_x, c_cat[...], TN, preferred_element_type=F32)
        spread = jnp.dot(hidden, down_cat[...], preferred_element_type=F32)
        spread_in = lax.dot_general(grad_x, up_cat[...], NT, preferred_element_type=F32)
        for k in range(slots):
            lanes = pl.ds(pl.multiple_of(index[n, k] * BLK, BLK), BLK)
            here = slice(k * BLK, (k + 1) * BLK)
            spot = k % 4 * 4 + p * 2
            grads[base + k // 4, spot] = jnp.where(k < live, up_grad[here, :], 0.0).astype(BF)
            grads[base + k // 4, spot + 1] = jnp.where(k < live, down_grad[:, here], 0.0).astype(BF)
            out_sum[:, lanes] += spread[:, here]
            in_sum[:, lanes] += spread_in[:, here]
        return carry

    lax.fori_loop(0, 4, one_panel, 0)
    leaving = []
    for n, hop in enumerate(HOPS[:7]):
        leaving.append(pltpu.make_async_copy(grads.at[(z + hop + NZ) % NZ], grads_out[n], grad_sems.at[n]))
    for o in range(2):
        spot = grads.at[(z + 4) % NZ, pl.ds(8 * o, 8)]
        leaving.append(pltpu.make_async_copy(spot, grads_out[7 + o], grad_sems.at[7 + o]))
    for copy in leaving:
        copy.start()
    for n, total_rows in enumerate((out_sum, in_sum)):
        for o in range(2):
            sums[2 * n + o] = total_rows[o * half : (o + 1) * half, :].astype(BF)
            copy = pltpu.make_async_copy(sums.at[2 * n + o], sums_out[2 * n + o], sum_sems.at[2 * n + o])
            copy.start()
            leaving.append(copy)
    for copy in leaving:
        copy.wait()


def products(place, index, count, act_pair, cot_pair, weights):
    panels, slots = index.shape
    half, features = act_pair[0].shape
    shard = weights[0].shape
    rows, wide = 2 * half, slots * BLK
    any_space = pl.BlockSpec(memory_space=pl.ANY)
    smem = pl.BlockSpec(memory_space=pltpu.SMEM)
    shapes = [part.shape for part in weights] + [(half, features)] * 4
    results = pl.pallas_call(
        functools.partial(products_kernel, slots),
        out_shape=[jax.ShapeDtypeStruct(shape, BF) for shape in shapes],
        in_specs=[smem] * 3 + [any_space] * 13,
        out_specs=[any_space] * 13,
        scratch_shapes=[
            pltpu.VMEM((rows, features), BF),
            pltpu.VMEM((rows, features), BF),
            pltpu.VMEM((NZ,) + shard, BF),
            pltpu.VMEM((NZ,) + shard, BF),
            pltpu.VMEM((rows, features), F32),
            pltpu.VMEM((rows, features), F32),
            pltpu.VMEM((4, half, features), BF),
            pltpu.VMEM((rows, wide), BF),
            pltpu.VMEM((rows, wide), BF),
            pltpu.VMEM((wide, BLK), BF),
            pltpu.VMEM((BLK, wide), BF),
            pltpu.SemaphoreType.DMA((4,)),
            pltpu.SemaphoreType.DMA((9,)),
            pltpu.SemaphoreType.DMA((9,)),
            pltpu.SemaphoreType.DMA((4,)),
        ],
        compiler_params=pltpu.CompilerParams(vmem_limit_bytes=60 * 2**20),
        cost_estimate=pl.CostEstimate(flops=1_700_000_000, bytes_accessed=16_000_000, transcendentals=65536),
    )(place, index, count, *act_pair, *cot_pair, *weights)
    return results[:9], results[9:]


def ring_gather(shard):
    up, down = [shard], [shard]
    for _ in range(3):
        up.append(send(up[-1], dz=-1))
        down.append(send(down[-1], dz=1))
    half = shard.shape[0] // 2
    across = [send(up[-1][:half], dz=-1), send(down[-1][half:], dz=1)]
    return [shard] + up[1:] + down[1:] + across


def pair(up, down):
    return send(up, dz=1), send(down, dz=-1)


def cut(value, parts):
    size = value.shape[0] // parts
    return [value[d * size : (d + 1) * size] for d in range(parts)]


def spread_rows(act, cot, ring, lists):
    act = [act] + [send(act, dx=-d) for d in (1, 2, 3)]
    cot = after(cot, *act[1:])
    cot = [cot] + [send(cot, dy=-d) for d in (1, 2, 3)]
    act, cot = after([jnp.concatenate(act), jnp.concatenate(cot)], lists)
    first = [send(act, dy=-1), send(act, dy=-3), send(cot, dx=-2)]
    act_2, cot_2 = after([act, cot], *first)
    second = [send(act_2, dy=-2), send(cot_2, dx=-1), send(cot_2, dx=-3)]
    first, second = after([first, second], ring[3], ring[6])
    act = jnp.concatenate([act, first[0], second[0], first[1]])
    cot = jnp.concatenate([cot, second[1], first[2], second[2]])
    return act, cot


def shards(activations, cotangent, up_panels, down_panels, block_index, block_count):
    row, col = lax.axis_index("row"), lax.axis_index("col")
    core, low, high = row % NC, row // NC, (col // NX) % NH
    own_first = core == 0

    lists = jnp.concatenate([block_index, block_count[:, None]], axis=1)
    far_lists = send(lists, dz=4)
    lists = lax.dynamic_slice_in_dim(jnp.stack([lists, far_lists]), 2 * core, 2, axis=1).reshape(4, -1)
    index, count = lists[:, :-1], lists[:, -1]
    place = (high * NL + low).astype(jnp.int32).reshape(1)

    both = jnp.stack([up_panels, down_panels], axis=2)
    keep = lax.dynamic_slice_in_dim(both, 2 * core, 2, axis=1)
    got = swap_cores(lax.dynamic_slice_in_dim(both, 2 - 2 * core, 2, axis=1))
    shard = jnp.where(own_first, jnp.stack([keep, got]), jnp.stack([got, keep]))
    weights = ring_gather(shard.reshape(-1, BLK, BLK))

    activations, cotangent = after([activations, cotangent], got)
    act, cot = spread_rows(activations, cotangent, weights, far_lists)
    act_pair, cot_pair = [act, swap_cores(act)], [cot, swap_cores(cot)]

    parts, (out_own, out_far, in_own, in_far) = products(place, index, count, act_pair, cot_pair, weights)
    step_1 = pair(parts[7], parts[8])
    up, down = cut(parts[3], 2), cut(parts[6], 2)
    up = jnp.concatenate([total([up[0], step_1[0]]).astype(BF), up[1]])
    down = jnp.concatenate([down[0], total([down[1], step_1[1]]).astype(BF)])
    step_2 = pair(up, down)

    out_far, in_far = swap_cores(out_far), swap_cores(in_far)
    out = [total(both).astype(BF) for both in zip(cut(out_own, 4), cut(out_far, 4))]
    gin = [total(both).astype(BF) for both in zip(cut(in_own, 4), cut(in_far, 4))]
    first = [send(out[1], dy=1), send(out[3], dy=3), send(gin[2], dx=2)]

    up = total([parts[2], step_2[0]]).astype(BF)
    down = total([parts[5], step_2[1]]).astype(BF)
    step_3 = pair(*after([up, down], *first))
    out_2, gin_1, gin_3 = after([out[2], gin[1], gin[3]], *first)
    second = [send(out_2, dy=2), send(gin_1, dx=1), send(gin_3, dx=3)]

    up = total([parts[1], step_3[0]]).astype(BF)
    down = total([parts[4], step_3[1]]).astype(BF)
    step_4 = pair(*after([up, down], *second))
    out = cut(total([out[0], first[0], first[1], second[0]]).astype(BF), 4)
    gin = cut(total([gin[0], second[1], second[2], first[2]]).astype(BF), 4)
    outputs = total([out[0]] + [send(out[d], dx=d) for d in (1, 2, 3)]).astype(BF)
    grad_inputs = total([gin[0]] + [send(gin[d], dy=d) for d in (1, 2, 3)]).astype(BF)

    cores = total([parts[0], *step_4]).astype(BF).reshape(2, 2, 2, 2, BLK, BLK)
    mine = lax.dynamic_index_in_dim(cores, core, 0, keepdims=False)
    other = swap_cores(lax.dynamic_index_in_dim(cores, 1 - core, 0, keepdims=False))
    grads = jnp.where(
        own_first, jnp.concatenate([mine, other], axis=1), jnp.concatenate([other, mine], axis=1)
    )
    return outputs, grad_inputs, grads[:, :, 0], grads[:, :, 1]


def solution(mesh):
    tokens = P(("row", "col"), None)
    blocks = P("row", "col", None, None)
    in_specs = (tokens, tokens, blocks, blocks, P("col", None), P("col"))
    out_specs = (tokens, tokens, blocks, blocks)
    return jax.shard_map(shards, mesh=mesh, in_specs=in_specs, out_specs=out_specs, check_vma=False)
```

```python
import functools

import jax
import jax.numpy as jnp
from jax import lax
from jax.experimental import pallas as pl
from jax.experimental.pallas import tpu as pltpu
from jax.sharding import PartitionSpec as P

BLK = 128
NX, NY, NH, NL, NC = 4, 4, 2, 4, 2
NZ = NH * NL
BF = jnp.bfloat16
F32 = jnp.float32
NT = (((1,), (1,)), ((), ()))
TN = (((0,), (0,)), ((), ()))
HOPS = (0, 1, 2, 3, -1, -2, -3, 4)


def device(z, core, y, x):
    z = z % NZ
    row = (z % NL) * NC + core % NC
    col = ((y % NY) * NH + z // NL) * NX + x % NX
    return row * NY * NH * NX + col


def send(value, dz=0, dc=0, dy=0, dx=0):
    pairs = [
        (device(z, c, y, x), device(z + dz, c + dc, y + dy, x + dx))
        for z in range(NZ)
        for c in range(NC)
        for y in range(NY)
        for x in range(NX)
    ]
    return lax.ppermute(value, ("row", "col"), pairs)


def swap_cores(value):
    return send(value, dc=1)


def after(values, *others):
    return lax.optimization_barrier((values, others))[0]


def total(terms):
    result = terms[0].astype(F32)
    for term in terms[1:]:
        result = result + term.astype(F32)
    return result


def products_kernel(slots, *refs):
    place, index, count = refs[:3]
    rows_in, weights_in = refs[3:5], refs[5:14]
    grads_out, sums_out = refs[14:23], refs[23:25]
    act, cot, weights, grads, out_sum, in_sum, sums, a_cat, c_cat, up_cat, down_cat = refs[25:36]
    row_sems, weight_sems, grad_sems, sum_sems = refs[36:]
    rows = act.shape[0]
    half = rows // 2
    z = place[0]
    own = z // NL
    hops = HOPS[:7] + (4, 4)
    arrivals = []
    for o in range(2):
        span = pl.ds(o * half, half)
        arrivals.append(pltpu.make_async_copy(rows_in[o].at[0], act.at[span], row_sems.at[o]))
        arrivals.append(pltpu.make_async_copy(rows_in[o].at[1], cot.at[span], row_sems.at[2 + o]))
    for copy in arrivals:
        copy.start()
    near, loads, stores = [], [], []
    for n, hop in enumerate(hops):
        there = (z + hop + NZ) % NZ
        spots = weights.at[there], grads.at[there]
        if hop == 4:
            spots = [spot.at[pl.ds(8 * (n - 7), 8)] for spot in spots]
        near.append(there // NL == own)
        loads.append(pltpu.make_async_copy(weights_in[n], spots[0], weight_sems.at[n]))
        stores.append(pltpu.make_async_copy(spots[1], grads_out[n], grad_sems.at[n]))
    for n in range(9):
        pl.when(near[n])(loads[n].start)
    for n in range(9):
        pl.when(jnp.logical_not(near[n]))(loads[n].start)
    out_sum[...] = jnp.zeros_like(out_sum)
    in_sum[...] = jnp.zeros_like(in_sum)
    for copy in arrivals:
        copy.wait()
    for n in range(9):
        pl.when(near[n])(loads[n].wait)
    leaving = []
    for n in range(4):
        far, p = n // 2, n % 2
        base = (1 - own if far else own) * NL
        live = count[n]
        if n == 2:
            for m in range(9):
                pl.when(jnp.logical_not(near[m]))(loads[m].wait)
                pl.when(near[m])(stores[m].start)
        for k in range(slots):
            lanes = pl.ds(pl.multiple_of(index[n, k] * BLK, BLK), BLK)
            here = slice(k * BLK, (k + 1) * BLK)
            a_cat[:, here] = act[:, lanes]
            c_cat[:, here] = cot[:, lanes]
            up = weights[base + k // 4, k % 4 * 4 + p * 2]
            down = weights[base + k // 4, k % 4 * 4 + p * 2 + 1]
            up_cat[here, :] = jnp.where(k < live, up, jnp.zeros_like(up))
            down_cat[:, here] = jnp.where(k < live, down, jnp.zeros_like(down))
        preact = jnp.dot(a_cat[...], up_cat[...], preferred_element_type=F32)
        grad_hidden = lax.dot_general(c_cat[...], down_cat[...], NT, preferred_element_type=F32)
        gate = jax.nn.sigmoid(preact)
        hidden = (preact * gate).astype(BF)
        derivative = gate * (1.0 + preact * (1.0 - gate))
        grad_pre = (grad_hidden * derivative).astype(BF)
        spread = jnp.dot(hidden, down_cat[...], preferred_element_type=F32)
        spread_in = lax.dot_general(grad_pre, up_cat[...], NT, preferred_element_type=F32)
        for k in range(slots):
            lanes = pl.ds(pl.multiple_of(index[n, k] * BLK, BLK), BLK)
            here = slice(k * BLK, (k + 1) * BLK)
            out_sum[:, lanes] += spread[:, here]
            in_sum[:, lanes] += spread_in[:, here]
        if n == 3:
            for o in (1, 0):
                for m, total_rows in enumerate((out_sum, in_sum)):
                    sums[o, m] = total_rows[o * half : (o + 1) * half, :].astype(BF)
                copy = pltpu.make_async_copy(sums.at[o], sums_out[o], sum_sems.at[o])
                copy.start()
                leaving.append(copy)
        up_grad = lax.dot_general(a_cat[...], grad_pre, TN, preferred_element_type=F32)
        down_grad = lax.dot_general(hidden, c_cat[...], TN, preferred_element_type=F32)
        for k in range(slots):
            here = slice(k * BLK, (k + 1) * BLK)
            spot = k % 4 * 4 + p * 2
            grads[base + k // 4, spot] = jnp.where(k < live, up_grad[here, :], 0.0).astype(BF)
            grads[base + k // 4, spot + 1] = jnp.where(k < live, down_grad[:, here], 0.0).astype(BF)
    for m in range(9):
        pl.when(jnp.logical_not(near[m]))(stores[m].start)
    for copy in leaving + stores:
        copy.wait()


def products(place, index, count, row_pair, weights):
    panels, slots = index.shape
    _, half, features = row_pair[0].shape
    shard = weights[0].shape
    rows, wide = 2 * half, slots * BLK
    any_space = pl.BlockSpec(memory_space=pl.ANY)
    smem = pl.BlockSpec(memory_space=pltpu.SMEM)
    shapes = [part.shape for part in weights] + [(2, half, features)] * 2
    results = pl.pallas_call(
        functools.partial(products_kernel, slots),
        out_shape=[jax.ShapeDtypeStruct(shape, BF) for shape in shapes],
        in_specs=[smem] * 3 + [any_space] * 11,
        out_specs=[any_space] * 11,
        scratch_shapes=[
            pltpu.VMEM((rows, features), BF),
            pltpu.VMEM((rows, features), BF),
            pltpu.VMEM((NZ,) + shard, BF),
            pltpu.VMEM((NZ,) + shard, BF),
            pltpu.VMEM((rows, features), F32),
            pltpu.VMEM((rows, features), F32),
            pltpu.VMEM((2, 2, half, features), BF),
            pltpu.VMEM((rows, wide), BF),
            pltpu.VMEM((rows, wide), BF),
            pltpu.VMEM((wide, BLK), BF),
            pltpu.VMEM((BLK, wide), BF),
            pltpu.SemaphoreType.DMA((4,)),
            pltpu.SemaphoreType.DMA((9,)),
            pltpu.SemaphoreType.DMA((9,)),
            pltpu.SemaphoreType.DMA((2,)),
        ],
        compiler_params=pltpu.CompilerParams(vmem_limit_bytes=60 * 2**20),
        cost_estimate=pl.CostEstimate(flops=1_700_000_000, bytes_accessed=16_000_000, transcendentals=65536),
    )(place, index, count, *row_pair, *weights)
    return results[:9], results[9:]


def ring_gather(shard):
    up, down = [shard], [shard]
    for _ in range(3):
        up.append(send(up[-1], dz=-1))
        down.append(send(down[-1], dz=1))
    half = shard.shape[0] // 2
    across = [send(up[-1][:half], dz=-1), send(down[-1][half:], dz=1)]
    return [shard] + up[1:] + down[1:] + across


def pair(up, down):
    return send(up, dz=1), send(down, dz=-1)


def cut(value, parts, axis=0):
    size = value.shape[axis] // parts
    return [lax.slice_in_dim(value, d * size, (d + 1) * size, axis=axis) for d in range(parts)]


def add_half(part, arrived, which):
    size = arrived.shape[0]
    room = [(which * size, (1 - which) * size)] + [(0, 0)] * (part.ndim - 1)
    return (part.astype(F32) + jnp.pad(arrived.astype(F32), room)).astype(BF)


def shards(activations, cotangent, up_panels, down_panels, block_index, block_count):
    row, col = lax.axis_index("row"), lax.axis_index("col")
    core, low, high = row % NC, row // NC, (col // NX) % NH
    own_first = core == 0

    lists = jnp.concatenate([block_index, block_count[:, None]], axis=1)
    far_lists = send(lists, dz=4)
    lists = lax.dynamic_slice_in_dim(jnp.stack([lists, far_lists]), 2 * core, 2, axis=1).reshape(4, -1)
    index, count = lists[:, :-1], lists[:, -1]
    place = (high * NL + low).astype(jnp.int32).reshape(1)

    both = jnp.stack([up_panels, down_panels], axis=2)
    keep = lax.dynamic_slice_in_dim(both, 2 * core, 2, axis=1)
    got = swap_cores(lax.dynamic_slice_in_dim(both, 2 - 2 * core, 2, axis=1))
    shard = jnp.where(own_first, jnp.stack([keep, got]), jnp.stack([got, keep]))
    weights = ring_gather(shard.reshape(-1, BLK, BLK))

    rows = jnp.stack([activations, cotangent])
    rows = [rows] + [send(rows, dx=-d) for d in (1, 2, 3)]
    rows = jnp.concatenate(after(rows, far_lists, weights[1], weights[4]), axis=1)
    rows = after([rows] + [send(rows, dy=-d) for d in (1, 2, 3)], weights[3], weights[6])
    rows = jnp.concatenate(rows, axis=1)
    row_pair = [rows, swap_cores(rows)]

    parts, (own, far) = products(place, index, count, row_pair, weights)
    step_1 = pair(parts[7], parts[8])
    up = add_half(parts[3], step_1[0], 0)
    down = add_half(parts[6], step_1[1], 1)
    step_2 = pair(up, down)

    far = swap_cores(far)
    sums = [total(both).astype(BF) for both in zip(cut(own, 4, 1), cut(far, 4, 1))]
    first = [send(sums[1], dy=1), send(sums[3], dy=3)]

    up = total([parts[2], step_2[0]]).astype(BF)
    down = total([parts[5], step_2[1]]).astype(BF)
    step_3 = pair(*after([up, down], *first))
    second = send(after(sums[2], *first), dy=2)

    up = total([parts[1], step_3[0]]).astype(BF)
    down = total([parts[4], step_3[1]]).astype(BF)
    step_4 = pair(*after([up, down], second))
    sums = after([sums[0], *first, second], *step_3)
    sums = cut(total(sums).astype(BF), 4, 1)
    sums = after([sums[0]] + [send(sums[d], dx=d) for d in (1, 2, 3)], *step_4)
    sums = total(sums).astype(BF)

    cores = total([parts[0], *step_4]).astype(BF).reshape(2, 2, 2, 2, BLK, BLK)
    mine = lax.dynamic_index_in_dim(cores, core, 0, keepdims=False)
    other = swap_cores(lax.dynamic_index_in_dim(cores, 1 - core, 0, keepdims=False))
    grads = jnp.where(
        own_first, jnp.concatenate([mine, other], axis=1), jnp.concatenate([other, mine], axis=1)
    )
    return sums[0], sums[1], grads[:, :, 0], grads[:, :, 1]


def solution(mesh):
    tokens = P(("row", "col"), None)
    blocks = P("row", "col", None, None)
    in_specs = (tokens, tokens, blocks, blocks, P("col", None), P("col"))
    out_specs = (tokens, tokens, blocks, blocks)
    return jax.shard_map(shards, mesh=mesh, in_specs=in_specs, out_specs=out_specs, check_vma=False)
```

```python
import functools

import jax
import jax.numpy as jnp
from jax import lax
from jax.experimental import pallas as pl
from jax.experimental.pallas import tpu as pltpu
from jax.sharding import PartitionSpec as P

BLK = 128
NX, NY, NH, NL, NC = 4, 4, 2, 4, 2
NZ = NH * NL
BF = jnp.bfloat16
F32 = jnp.float32
NT = (((1,), (1,)), ((), ()))
TN = (((0,), (0,)), ((), ()))
HOPS = (0, 1, 2, 3, -1, -2, -3, 4)
LIST_ROWS = 16


def device(z, core, y, x):
    z = z % NZ
    row = (z % NL) * NC + core % NC
    col = ((y % NY) * NH + z // NL) * NX + x % NX
    return row * NY * NH * NX + col


def send(value, dz=0, dc=0, dy=0, dx=0):
    pairs = [
        (device(z, c, y, x), device(z + dz, c + dc, y + dy, x + dx))
        for z in range(NZ)
        for c in range(NC)
        for y in range(NY)
        for x in range(NX)
    ]
    return lax.ppermute(value, ("row", "col"), pairs)


def swap_cores(value):
    return send(value, dc=1)


def after(values, *others):
    return lax.optimization_barrier((values, others))[0]


def total(terms):
    result = terms[0].astype(F32)
    for term in terms[1:]:
        result = result + term.astype(F32)
    return result


def products_kernel(slots, *refs):
    place, index, count = refs[:3]
    rows_in, weights_in = refs[3:5], refs[5:14]
    grads_out, sums_out = refs[14:23], refs[23:25]
    act, cot, weights, grads, out_sum, in_sum, sums, *cats = refs[25:36]
    row_sems, weight_sems, grad_sems, sum_sems = refs[36:]
    rows = act.shape[0]
    half = rows // 2
    z = place[0]
    own = z // NL
    hops = HOPS[:7] + (4, 4)
    arrivals = []
    for o in range(2):
        span = pl.ds(o * half, half)
        arrivals.append(pltpu.make_async_copy(rows_in[o].at[0], act.at[span], row_sems.at[o]))
        arrivals.append(pltpu.make_async_copy(rows_in[o].at[1], cot.at[span], row_sems.at[2 + o]))
    for copy in arrivals:
        copy.start()
    size = weights.shape[1]
    near, loads, stores = [], [], []
    for n, hop in enumerate(hops):
        there = (z + hop + NZ) % NZ
        near.append(there // NL == own)
        if hop == 4:
            first = n - 7
            source, spot = weights_in[n], weights.at[there, pl.ds(first * (size // 2), size // 2)]
            result = grads.at[there, pl.ds(8 * first, 8)]
        else:
            source, spot = weights_in[n].at[pl.ds(0, size)], weights.at[there]
            result = grads.at[there]
        loads.append(pltpu.make_async_copy(source, spot, weight_sems.at[n]))
        stores.append(pltpu.make_async_copy(result, grads_out[n], grad_sems.at[n]))
    for n in range(9):
        pl.when(near[n])(loads[n].start)
    for n in range(9):
        pl.when(jnp.logical_not(near[n]))(loads[n].start)
    out_sum[...] = jnp.zeros_like(out_sum)
    in_sum[...] = jnp.zeros_like(in_sum)
    for copy in arrivals:
        copy.wait()
    for n in range(9):
        pl.when(near[n])(loads[n].wait)
    leaving = []
    for n in range(4):
        far, p = n // 2, n % 2
        base = (1 - own if far else own) * NL
        live = count[n]
        a_cat, c_cat, up_cat, down_cat = [cat.at[n % 2] for cat in cats]
        if n == 2:
            for m in range(9):
                pl.when(jnp.logical_not(near[m]))(loads[m].wait)
                pl.when(near[m])(stores[m].start)
        for k in range(slots):
            lanes = pl.ds(pl.multiple_of(index[n, k] * BLK, BLK), BLK)
            here = slice(k * BLK, (k + 1) * BLK)
            a_cat[:, here] = act[:, lanes]
            c_cat[:, here] = cot[:, lanes]
            spot = (k % 4 * 4 + p * 2) * BLK
            up = weights[base + k // 4, spot : spot + BLK]
            down = weights[base + k // 4, spot + BLK : spot + 2 * BLK]
            up_cat[here, :] = jnp.where(k < live, up, jnp.zeros_like(up))
            down_cat[:, here] = jnp.where(k < live, down, jnp.zeros_like(down))
        preact = jnp.dot(a_cat[...], up_cat[...], preferred_element_type=F32)
        grad_hidden = lax.dot_general(c_cat[...], down_cat[...], NT, preferred_element_type=F32)
        gate = jax.nn.sigmoid(preact)
        hidden = (preact * gate).astype(BF)
        derivative = gate * (1.0 + preact * (1.0 - gate))
        grad_pre = (grad_hidden * derivative).astype(BF)
        spread = jnp.dot(hidden, down_cat[...], preferred_element_type=F32)
        spread_in = lax.dot_general(grad_pre, up_cat[...], NT, preferred_element_type=F32)
        for k in range(slots):
            lanes = pl.ds(pl.multiple_of(index[n, k] * BLK, BLK), BLK)
            here = slice(k * BLK, (k + 1) * BLK)
            out_sum[:, lanes] += spread[:, here]
            in_sum[:, lanes] += spread_in[:, here]
        if n == 3:
            for o in (1, 0):
                for m, total_rows in enumerate((out_sum, in_sum)):
                    sums[o, m] = total_rows[o * half : (o + 1) * half, :].astype(BF)
                copy = pltpu.make_async_copy(sums.at[o], sums_out[o], sum_sems.at[o])
                copy.start()
                leaving.append(copy)
        up_grad = lax.dot_general(a_cat[...], grad_pre, TN, preferred_element_type=F32)
        down_grad = lax.dot_general(hidden, c_cat[...], TN, preferred_element_type=F32)
        for k in range(slots):
            here = slice(k * BLK, (k + 1) * BLK)
            spot = k % 4 * 4 + p * 2
            grads[base + k // 4, spot] = jnp.where(k < live, up_grad[here, :], 0.0).astype(BF)
            grads[base + k // 4, spot + 1] = jnp.where(k < live, down_grad[:, here], 0.0).astype(BF)
    for m in range(9):
        pl.when(jnp.logical_not(near[m]))(stores[m].start)
    for copy in leaving + stores:
        copy.wait()


def products(place, index, count, row_pair, weights):
    panels, slots = index.shape
    _, half, features = row_pair[0].shape
    size = 2 * weights[7].shape[0]
    blocks = size // BLK
    rows, wide = 2 * half, slots * BLK
    any_space = pl.BlockSpec(memory_space=pl.ANY)
    smem = pl.BlockSpec(memory_space=pltpu.SMEM)
    shapes = [(blocks, BLK, BLK)] * 7 + [(blocks // 2, BLK, BLK)] * 2 + [(2, half, features)] * 2
    results = pl.pallas_call(
        functools.partial(products_kernel, slots),
        out_shape=[jax.ShapeDtypeStruct(shape, BF) for shape in shapes],
        in_specs=[smem] * 3 + [any_space] * 11,
        out_specs=[any_space] * 11,
        scratch_shapes=[
            pltpu.VMEM((rows, features), BF),
            pltpu.VMEM((rows, features), BF),
            pltpu.VMEM((NZ, size, BLK), BF),
            pltpu.VMEM((NZ, blocks, BLK, BLK), BF),
            pltpu.VMEM((rows, features), F32),
            pltpu.VMEM((rows, features), F32),
            pltpu.VMEM((2, 2, half, features), BF),
            pltpu.VMEM((2, rows, wide), BF),
            pltpu.VMEM((2, rows, wide), BF),
            pltpu.VMEM((2, wide, BLK), BF),
            pltpu.VMEM((2, BLK, wide), BF),
            pltpu.SemaphoreType.DMA((4,)),
            pltpu.SemaphoreType.DMA((9,)),
            pltpu.SemaphoreType.DMA((9,)),
            pltpu.SemaphoreType.DMA((2,)),
        ],
        compiler_params=pltpu.CompilerParams(vmem_limit_bytes=60 * 2**20),
        cost_estimate=pl.CostEstimate(flops=1_700_000_000, bytes_accessed=16_000_000, transcendentals=65536),
    )(place, index, count, *row_pair, *weights)
    return results[:9], results[9:]


def pair(up, down):
    return send(up, dz=1), send(down, dz=-1)


def cut(value, parts, axis=0):
    size = value.shape[axis] // parts
    return [lax.slice_in_dim(value, d * size, (d + 1) * size, axis=axis) for d in range(parts)]


def add_half(part, arrived, which):
    size = arrived.shape[0]
    room = [(which * size, (1 - which) * size)] + [(0, 0)] * (part.ndim - 1)
    return (part.astype(F32) + jnp.pad(arrived.astype(F32), room)).astype(BF)


def shards(activations, cotangent, up_panels, down_panels, block_index, block_count):
    row, col = lax.axis_index("row"), lax.axis_index("col")
    core, low, high = row % NC, row // NC, (col // NX) % NH
    own_first = core == 0

    place = (high * NL + low).astype(jnp.int32).reshape(1)

    both = jnp.stack([up_panels, down_panels], axis=2)
    keep = lax.dynamic_slice_in_dim(both, 2 * core, 2, axis=1)
    got = swap_cores(lax.dynamic_slice_in_dim(both, 2 - 2 * core, 2, axis=1))
    shard = jnp.where(own_first, jnp.stack([keep, got]), jnp.stack([got, keep])).reshape(-1, BLK)
    lists = jnp.concatenate([block_index, block_count[:, None]], axis=1)
    row_of_lists = lists.reshape(1, -1).astype(BF)
    row_of_lists = jnp.pad(row_of_lists, ((0, LIST_ROWS - 1), (0, BLK - row_of_lists.shape[1])))
    shard = jnp.concatenate([shard, row_of_lists])
    ring_1 = send(shard, dz=-1), send(shard, dz=1)
    rows = jnp.stack([activations, cotangent])
    rows = [rows] + [send(rows, dx=-d) for d in (1, 2, 3)]
    rows = jnp.concatenate(after(rows, *ring_1), axis=1)
    up, down = after(ring_1, rows)
    ring_2 = send(up, dz=-1), send(down, dz=1)
    size = shard.shape[0] - LIST_ROWS
    ring_3 = send(ring_2[0][:size], dz=-1), send(ring_2[1][:size], dz=1)
    ring_4 = send(ring_3[0][: size // 2], dz=-1), send(ring_3[1][size // 2 :], dz=1)
    weights = [shard, ring_1[0], ring_2[0], ring_3[0], ring_1[1], ring_2[1], ring_3[1], *ring_4]
    rows = after([rows] + [send(rows, dy=-d) for d in (1, 2, 3)], *ring_3)
    rows = jnp.concatenate(rows, axis=1)
    row_pair = [rows, swap_cores(rows)]

    below, above = [v[1][-LIST_ROWS] for v in (ring_1, ring_2)], [v[0][-LIST_ROWS] for v in (ring_2, ring_1)]
    far_lists = jnp.where(low < 2, jnp.where(low == 0, *below), jnp.where(low == 2, *above))
    far_lists = far_lists[: lists.size]
    far_lists = far_lists.astype(jnp.int32).reshape(lists.shape)
    lists = lax.dynamic_slice_in_dim(jnp.stack([lists, far_lists]), 2 * core, 2, axis=1).reshape(4, -1)
    index, count = lists[:, :-1], lists[:, -1]

    parts, (own, far) = products(place, index, count, row_pair, weights)
    step_1 = pair(parts[7], parts[8])
    up = add_half(parts[3], step_1[0], 0)
    down = add_half(parts[6], step_1[1], 1)
    step_2 = pair(up, down)

    far = swap_cores(far)
    sums = [total(both).astype(BF) for both in zip(cut(own, 4, 1), cut(far, 4, 1))]
    first = [send(sums[1], dy=1), send(sums[3], dy=3)]

    up = total([parts[2], step_2[0]]).astype(BF)
    down = total([parts[5], step_2[1]]).astype(BF)
    step_3 = pair(*after([up, down], *first))
    second = send(after(sums[2], *first), dy=2)

    up = total([parts[1], step_3[0]]).astype(BF)
    down = total([parts[4], step_3[1]]).astype(BF)
    step_4 = pair(*after([up, down], second))
    sums = after([sums[0], *first, second], *step_3)
    sums = cut(total(sums).astype(BF), 4, 1)
    sums = after([sums[0]] + [send(sums[d], dx=d) for d in (1, 2, 3)], *step_4)
    sums = total(sums).astype(BF)

    cores = total([parts[0], *step_4]).astype(BF).reshape(2, 2, 2, 2, BLK, BLK)
    mine = lax.dynamic_index_in_dim(cores, core, 0, keepdims=False)
    other = swap_cores(lax.dynamic_index_in_dim(cores, 1 - core, 0, keepdims=False))
    grads = jnp.where(
        own_first, jnp.concatenate([mine, other], axis=1), jnp.concatenate([other, mine], axis=1)
    )
    return sums[0], sums[1], grads[:, :, 0], grads[:, :, 1]


def solution(mesh):
    tokens = P(("row", "col"), None)
    blocks = P("row", "col", None, None)
    in_specs = (tokens, tokens, blocks, blocks, P("col", None), P("col"))
    out_specs = (tokens, tokens, blocks, blocks)
    return jax.shard_map(shards, mesh=mesh, in_specs=in_specs, out_specs=out_specs, check_vma=False)
```

```python
import functools

import jax
import jax.numpy as jnp
from jax import lax
from jax.experimental import pallas as pl
from jax.experimental.pallas import tpu as pltpu
from jax.sharding import PartitionSpec as P

BLK = 128
NX, NY, NH, NL, NC = 4, 4, 2, 4, 2
NZ = NH * NL
BF = jnp.bfloat16
F32 = jnp.float32
NT = (((1,), (1,)), ((), ()))
TN = (((0,), (0,)), ((), ()))
HOPS = (0, 1, 2, 3, -1, -2, -3, 4)
LIST_ROWS = 16


def device(z, core, y, x):
    z = z % NZ
    row = (z % NL) * NC + core % NC
    col = ((y % NY) * NH + z // NL) * NX + x % NX
    return row * NY * NH * NX + col


def send(value, dz=0, dc=0, dy=0, dx=0):
    pairs = [
        (device(z, c, y, x), device(z + dz, c + dc, y + dy, x + dx))
        for z in range(NZ)
        for c in range(NC)
        for y in range(NY)
        for x in range(NX)
    ]
    return lax.ppermute(value, ("row", "col"), pairs)


def swap_cores(value):
    return send(value, dc=1)


def after(values, *others):
    return lax.optimization_barrier((values, others))[0]


def total(terms):
    result = terms[0].astype(F32)
    for term in terms[1:]:
        result = result + term.astype(F32)
    return result


def products_kernel(slots, *refs):
    place, index, count = refs[:3]
    rows_in, weights_in = refs[3:5], refs[5:14]
    grads_out, sums_out = refs[14:23], refs[23:25]
    act, cot, weights, grads, out_sum, in_sum, sums, *cats = refs[25:36]
    row_sems, weight_sems, grad_sems, sum_sems = refs[36:]
    rows = act.shape[0]
    half = rows // 2
    z = place[0]
    own = z // NL
    hops = HOPS[:7] + (4, 4)
    arrivals = []
    for o in range(2):
        span = pl.ds(o * half, half)
        arrivals.append(pltpu.make_async_copy(rows_in[o].at[0], act.at[span], row_sems.at[o]))
        arrivals.append(pltpu.make_async_copy(rows_in[o].at[1], cot.at[span], row_sems.at[2 + o]))
    for copy in arrivals:
        copy.start()
    size = weights.shape[1]
    near, loads, stores = [], [], []
    for n, hop in enumerate(hops):
        there = (z + hop + NZ) % NZ
        near.append(there // NL == own)
        if hop == 4:
            first = n - 7
            source, spot = weights_in[n], weights.at[there, pl.ds(first * (size // 2), size // 2)]
            result = grads.at[there, pl.ds(8 * first, 8)]
        else:
            source, spot = weights_in[n].at[pl.ds(0, size)], weights.at[there]
            result = grads.at[there]
        loads.append(pltpu.make_async_copy(source, spot, weight_sems.at[n]))
        stores.append(pltpu.make_async_copy(result, grads_out[n], grad_sems.at[n]))
    for n in range(9):
        pl.when(near[n])(loads[n].start)
    for n in range(9):
        pl.when(jnp.logical_not(near[n]))(loads[n].start)
    out_sum[...] = jnp.zeros_like(out_sum)
    in_sum[...] = jnp.zeros_like(in_sum)
    for copy in arrivals:
        copy.wait()
    for n in range(9):
        pl.when(near[n])(loads[n].wait)
    leaving = []
    for n in range(4):
        far, p = n // 2, n % 2
        base = (1 - own if far else own) * NL
        live = count[n]
        a_cat, c_cat, up_cat, down_cat = [cat.at[n % 2] for cat in cats]
        if n == 2:
            for m in range(9):
                pl.when(jnp.logical_not(near[m]))(loads[m].wait)
                pl.when(near[m])(stores[m].start)
        for k in range(slots):
            lanes = pl.ds(pl.multiple_of(index[n, k] * BLK, BLK), BLK)
            here = slice(k * BLK, (k + 1) * BLK)
            a_cat[:, here] = act[:, lanes]
            c_cat[:, here] = cot[:, lanes]
            spot = (k % 4 * 4 + p * 2) * BLK
            up = weights[base + k // 4, spot : spot + BLK]
            down = weights[base + k // 4, spot + BLK : spot + 2 * BLK]
            up_cat[here, :] = jnp.where(k < live, up, jnp.zeros_like(up))
            down_cat[:, here] = jnp.where(k < live, down, jnp.zeros_like(down))
        preact = jnp.dot(a_cat[...], up_cat[...], preferred_element_type=F32)
        grad_hidden = lax.dot_general(c_cat[...], down_cat[...], NT, preferred_element_type=F32)
        gate = jax.nn.sigmoid(preact)
        hidden = (preact * gate).astype(BF)
        derivative = gate * (1.0 + preact * (1.0 - gate))
        grad_pre = (grad_hidden * derivative).astype(BF)
        spread = jnp.dot(hidden, down_cat[...], preferred_element_type=F32)
        spread_in = lax.dot_general(grad_pre, up_cat[...], NT, preferred_element_type=F32)
        for k in range(slots):
            lanes = pl.ds(pl.multiple_of(index[n, k] * BLK, BLK), BLK)
            here = slice(k * BLK, (k + 1) * BLK)
            out_sum[:, lanes] += spread[:, here]
            in_sum[:, lanes] += spread_in[:, here]
        if n == 3:
            for o in (1, 0):
                for m, total_rows in enumerate((out_sum, in_sum)):
                    sums[o, m] = total_rows[o * half : (o + 1) * half, :].astype(BF)
                copy = pltpu.make_async_copy(sums.at[o], sums_out[o], sum_sems.at[o])
                copy.start()
                leaving.append(copy)
        up_grad = lax.dot_general(a_cat[...], grad_pre, TN, preferred_element_type=F32)
        down_grad = lax.dot_general(hidden, c_cat[...], TN, preferred_element_type=F32)
        for k in range(slots):
            here = slice(k * BLK, (k + 1) * BLK)
            spot = k % 4 * 4 + p * 2
            grads[base + k // 4, spot] = jnp.where(k < live, up_grad[here, :], 0.0).astype(BF)
            grads[base + k // 4, spot + 1] = jnp.where(k < live, down_grad[:, here], 0.0).astype(BF)
    for m in range(9):
        pl.when(jnp.logical_not(near[m]))(stores[m].start)
    for copy in leaving + stores:
        copy.wait()


def products(place, index, count, row_pair, weights):
    panels, slots = index.shape
    _, half, features = row_pair[0].shape
    size = 2 * weights[7].shape[0]
    blocks = size // BLK
    rows, wide = 2 * half, slots * BLK
    any_space = pl.BlockSpec(memory_space=pl.ANY)
    smem = pl.BlockSpec(memory_space=pltpu.SMEM)
    shapes = [(blocks, BLK, BLK)] * 7 + [(blocks // 2, BLK, BLK)] * 2 + [(2, half, features)] * 2
    results = pl.pallas_call(
        functools.partial(products_kernel, slots),
        out_shape=[jax.ShapeDtypeStruct(shape, BF) for shape in shapes],
        in_specs=[smem] * 3 + [any_space] * 11,
        out_specs=[any_space] * 11,
        scratch_shapes=[
            pltpu.VMEM((rows, features), BF),
            pltpu.VMEM((rows, features), BF),
            pltpu.VMEM((NZ, size, BLK), BF),
            pltpu.VMEM((NZ, blocks, BLK, BLK), BF),
            pltpu.VMEM((rows, features), F32),
            pltpu.VMEM((rows, features), F32),
            pltpu.VMEM((2, 2, half, features), BF),
            pltpu.VMEM((2, rows, wide), BF),
            pltpu.VMEM((2, rows, wide), BF),
            pltpu.VMEM((2, wide, BLK), BF),
            pltpu.VMEM((2, BLK, wide), BF),
            pltpu.SemaphoreType.DMA((4,)),
            pltpu.SemaphoreType.DMA((9,)),
            pltpu.SemaphoreType.DMA((9,)),
            pltpu.SemaphoreType.DMA((2,)),
        ],
        compiler_params=pltpu.CompilerParams(vmem_limit_bytes=60 * 2**20),
        cost_estimate=pl.CostEstimate(flops=1_700_000_000, bytes_accessed=16_000_000, transcendentals=65536),
    )(place, index, count, *row_pair, *weights)
    return results[:9], results[9:]


def pair(up, down):
    return send(up, dz=1), send(down, dz=-1)


def cut(value, parts, axis=0):
    size = value.shape[axis] // parts
    return [lax.slice_in_dim(value, d * size, (d + 1) * size, axis=axis) for d in range(parts)]


def add_half(part, arrived, which):
    size = arrived.shape[0]
    room = [(which * size, (1 - which) * size)] + [(0, 0)] * (part.ndim - 1)
    return (part.astype(F32) + jnp.pad(arrived.astype(F32), room)).astype(BF)


def shards(activations, cotangent, up_panels, down_panels, block_index, block_count):
    row, col = lax.axis_index("row"), lax.axis_index("col")
    core, low, high = row % NC, row // NC, (col // NX) % NH
    own_first = core == 0

    place = (high * NL + low).astype(jnp.int32).reshape(1)

    both = jnp.stack([up_panels, down_panels], axis=2)
    keep = lax.dynamic_slice_in_dim(both, 2 * core, 2, axis=1)
    got = swap_cores(lax.dynamic_slice_in_dim(both, 2 - 2 * core, 2, axis=1))
    shard = jnp.where(own_first, jnp.stack([keep, got]), jnp.stack([got, keep])).reshape(-1, BLK)
    lists = jnp.concatenate([block_index, block_count[:, None]], axis=1)
    row_of_lists = lists.reshape(1, -1).astype(BF)
    row_of_lists = jnp.pad(row_of_lists, ((0, LIST_ROWS - 1), (0, BLK - row_of_lists.shape[1])))
    shard = jnp.concatenate([shard, row_of_lists])
    ring_1 = send(shard, dz=-1), send(shard, dz=1)
    rows = jnp.stack([activations, cotangent])
    rows = [rows] + [send(rows, dx=-d) for d in (1, 2, 3)]
    rows = jnp.concatenate(after(rows, *ring_1), axis=1)
    up, down = after(ring_1, rows)
    ring_2 = send(up, dz=-1), send(down, dz=1)
    size = shard.shape[0] - LIST_ROWS
    below, above = [v[1][-LIST_ROWS] for v in (ring_1, ring_2)], [v[0][-LIST_ROWS] for v in (ring_2, ring_1)]
    far_lists = jnp.where(low < 2, jnp.where(low == 0, *below), jnp.where(low == 2, *above))
    far_lists = far_lists[: lists.size]
    up, down = after(ring_2, far_lists)
    ring_3 = send(up[:size], dz=-1), send(down[:size], dz=1)
    ring_4 = send(ring_3[0][: size // 2], dz=-1), send(ring_3[1][size // 2 :], dz=1)
    weights = [shard, ring_1[0], ring_2[0], ring_3[0], ring_1[1], ring_2[1], ring_3[1], *ring_4]
    rows = after([rows] + [send(rows, dy=-d) for d in (1, 2, 3)], *ring_3)
    rows = jnp.concatenate(rows, axis=1)
    row_pair = [rows, swap_cores(rows)]

    far_lists = far_lists.astype(jnp.int32).reshape(lists.shape)
    lists = lax.dynamic_slice_in_dim(jnp.stack([lists, far_lists]), 2 * core, 2, axis=1).reshape(4, -1)
    index, count = lists[:, :-1], lists[:, -1]

    parts, (own, far) = products(place, index, count, row_pair, weights)
    step_1 = pair(parts[7], parts[8])
    up = add_half(parts[3], step_1[0], 0)
    down = add_half(parts[6], step_1[1], 1)
    step_2 = pair(up, down)

    far = swap_cores(far)
    sums = [total(both).astype(BF) for both in zip(cut(own, 4, 1), cut(far, 4, 1))]
    first = [send(sums[1], dy=1), send(sums[3], dy=3)]

    up = total([parts[2], step_2[0]]).astype(BF)
    down = total([parts[5], step_2[1]]).astype(BF)
    step_3 = pair(*after([up, down], *first))
    second = send(after(sums[2], *first), dy=2)

    up = total([parts[1], step_3[0]]).astype(BF)
    down = total([parts[4], step_3[1]]).astype(BF)
    step_4 = pair(*after([up, down], second))
    sums = after([sums[0], *first, second], *step_3)
    sums = cut(total(sums).astype(BF), 4, 1)
    sums = after([sums[0]] + [send(sums[d], dx=d) for d in (1, 2, 3)], *step_4)
    sums = total(sums).astype(BF)

    cores = total([parts[0], *step_4]).astype(BF).reshape(2, 2, 2, 2, BLK, BLK)
    mine = lax.dynamic_index_in_dim(cores, core, 0, keepdims=False)
    other = swap_cores(lax.dynamic_index_in_dim(cores, 1 - core, 0, keepdims=False))
    grads = jnp.where(
        own_first, jnp.concatenate([mine, other], axis=1), jnp.concatenate([other, mine], axis=1)
    )
    return sums[0], sums[1], grads[:, :, 0], grads[:, :, 1]


def solution(mesh):
    tokens = P(("row", "col"), None)
    blocks = P("row", "col", None, None)
    in_specs = (tokens, tokens, blocks, blocks, P("col", None), P("col"))
    out_specs = (tokens, tokens, blocks, blocks)
    return jax.shard_map(shards, mesh=mesh, in_specs=in_specs, out_specs=out_specs, check_vma=False)
```
